128 devices in a mesh: dp: 4 (over z), tensor: 32 (over x, y, core).
Axes of the slice: x: 4, y: 4, z: 4, core: 2. Of those that a mesh axis runs over, the one named last changes fastest.
Arguments:
- grads: bfloat16 [4, 2, 8192, 8192], P('dp', None, 'tensor'), may hold values from -60 to 60, as said below
- error: bfloat16 [4, 2, 8192, 8192], P('dp', None, 'tensor'), may hold values from -3 to 3
- q_init: float32 [2, 8192, 32], P(None, 'tensor'), may hold values from -6 to 6
Outputs:
- new_error: bfloat16 [4, 2, 8192, 8192], P('dp', None, 'tensor')
- p_factor: float32 [2, 8192, 32], P(None, 'tensor')
- q_factor: float32 [2, 8192, 32], P(None, 'tensor')
The draws below stay inside these ranges and needn't reach their ends.
Inputs may be any that keep to these rules, and one draw needn't show every extreme that they name: `grads`: entries of order one, rows of different scales.
All inputs are finite; a program needn't handle non-finite values.
Results may differ from the reference program's by a relative error of at most 0.018.
Values may be sent and summed in bfloat16 or wider, within the bound.
A program may use at most 128 MiB of HBM per device.

```python
import math
import jax
import jax.numpy as jnp
from jax import lax

ROWS = 8192
COLS = 8192
RANK = 32
MATS = 2
ITERS = 2
REPLICAS = 4


def draw_grads(key, part):
    key = jax.random.fold_in(key, 5)
    key_own, key_scale = jax.random.split(key, 2)
    shape = (REPLICAS, MATS, ROWS, COLS)
    position = jnp.arange(ROWS, dtype=jnp.float32) / ROWS
    rising = (1.0 + 2.0 * position)[:, None]
    row_scale = jnp.exp(jax.random.uniform(key_scale, (REPLICAS, MATS, ROWS, 1), jnp.float32) * math.log(10.0))
    row_scale = row_scale * rising
    base = jnp.clip(jax.random.normal(key_own, shape, jnp.float32), -6.0, 6.0)
    return (base * row_scale * 0.25).astype(jnp.bfloat16)


def block_scale(key, extent, pieces, least, high):
    factor_of, own = 1.0, jax.random.fold_in(key, 6)
    for dim, shards_of in pieces:
        draws = jnp.exp(jax.random.uniform(jax.random.fold_in(own, dim), (shards_of,), jnp.float32, least / len(pieces), high / len(pieces)))
        factor_of = factor_of * jnp.repeat(draws, extent[dim] // shards_of).reshape([-1 if axis == dim else 1 for axis in range(len(extent))])
    return factor_of


def normal_values(rng, dims, deviation, most, cuts=(), held_as=jnp.bfloat16):
    entries = deviation * jax.random.normal(rng, dims, jnp.float32)
    if cuts:
        entries = entries * block_scale(rng, dims, cuts, -0.22, 0.18)
    return jnp.clip(entries, -most, most).astype(held_as)


def setup_inputs(seed: int = 0) -> dict:
    seeds = jax.random.split(jax.random.key(seed), 4)
    return {
        "grads": draw_grads(jax.random.fold_in(seeds[3], 71), 0),
        "error": normal_values(seeds[1], (REPLICAS, MATS, ROWS, COLS), 0.5, 3.0, ((0, 4), (2, 32))),
        "q_init": normal_values(seeds[2], (MATS, COLS, RANK), 1.0, 6.0, ((1, 32),), jnp.float32),
    }


def orthonormal(left):
    gram_sum = jnp.einsum('mrk,mrj->mkj', left, left, precision=lax.Precision.HIGHEST)
    cholesky_factor = jnp.linalg.cholesky(gram_sum)

    def solve_one(factor, block):
        return jax.scipy.linalg.solve_triangular(factor, block.T, lower=True).T
    return jax.vmap(solve_one)(cholesky_factor, left)

def rounded(values):
    return lax.optimization_barrier(values.astype(jnp.bfloat16)).astype(jnp.float32)

def reference(grads, error, q_init):
    shrink_by = 1.0 / REPLICAS

    def merged_of(replica):
        return (grads[replica].astype(jnp.float32) + error[replica].astype(jnp.float32)).astype(jnp.bfloat16)
    right = q_init
    basis = None
    for sweep in range(ITERS):
        right_bf = rounded(right)

        def add_left(total, replica):
            merged = merged_of(replica).astype(jnp.float32)
            return (total + jnp.einsum('mrc,mck->mrk', merged, right_bf, precision=lax.Precision.HIGHEST), None)
        left, _ = lax.scan(add_left, jnp.zeros((MATS, ROWS, RANK), jnp.float32), jnp.arange(REPLICAS))
        left = left * shrink_by
        basis = orthonormal(left)
        basis_bf = rounded(basis)

        def add_right(total, replica):
            merged = merged_of(replica).astype(jnp.float32)
            return (total + jnp.einsum('mrc,mrk->mck', merged, basis_bf, precision=lax.Precision.HIGHEST), None)
        right, _ = lax.scan(add_right, jnp.zeros((MATS, COLS, RANK), jnp.float32), jnp.arange(REPLICAS))
        right = right * shrink_by
    low_rank = jnp.einsum('mrk,mck->mrc', basis, right, precision=lax.Precision.HIGHEST)

    def fresh_error(replica):
        return (merged_of(replica).astype(jnp.float32) - low_rank).astype(jnp.bfloat16)
    new_error = lax.map(fresh_error, jnp.arange(REPLICAS))
    return (new_error, basis * math.sqrt(ROWS), right)
```

```python
import functools
import math

import jax
import jax.numpy as jnp
from jax import lax
from jax.experimental import pallas as pl
from jax.experimental.pallas import tpu as pltpu
from jax.sharding import PartitionSpec as P

ITERS = 2
BF = jnp.bfloat16
F32 = jnp.float32
MESH = pl.DeviceIdType.MESH
HIGHEST = lax.Precision.HIGHEST
RING = (2, 1, 3, 0)
FAR_FIRST = tuple(
    sorted(
        ((dx, dy) for dx in range(4) for dy in range(4) if dx or dy),
        key=lambda s: -(min(s[0], 4 - s[0]) + min(s[1], 4 - s[1])),
    )
)
NEAR_FIRST = FAR_FIRST[::-1]
LOADS = 4


def nt(a, b, **kw):
    return lax.dot_general(a, b, (((1,), (1,)), ((), ())), preferred_element_type=F32, **kw)


def nn(a, b, **kw):
    return lax.dot_general(a, b, (((1,), (0,)), ((), ())), preferred_element_type=F32, **kw)


def inverse_factor(gram):
    n = gram.shape[0]
    row = lax.broadcasted_iota(jnp.int32, (n, 4 * n), 0)
    lane = lax.broadcasted_iota(jnp.int32, (n, 4 * n), 1)
    work = jnp.where(lane == row + n, 1.0, gram)
    for j in range(n):
        column = jnp.broadcast_to(work[:, j : j + 1], work.shape)
        pivot = jnp.broadcast_to(column[j : j + 1, :], work.shape)
        line = jnp.broadcast_to(work[j : j + 1, :], work.shape)
        work = work - jnp.where(row > j, column / pivot, 0.0) * line
    diagonal = jnp.sum(jnp.where(lane == row, work, 0.0), axis=1, keepdims=True)
    work = work * lax.rsqrt(diagonal)
    return work[:, n : 2 * n]


def factors_kernel(
    grads, error, q_init, merged, right_out, basis_out,
    error_vm, q_vm, right_in, left_part, left_sum, left_bf, part, part_in, chip_sum, plane_in,
    z_in, gram_own, gram_core, gram_in, inv_own, q_stage,
    load_sem, q_load_sem, q_core_sem, ag_send, ag_recv, fwd_send, fwd_recv,
    left_send, left_recv, core_send, core_recv, rs_send, rs_recv, z_send, z_recv,
    gc_sem, g_send, g_recv, inv_sem,
):
    z = lax.axis_index("dp")
    t = lax.axis_index("tensor")
    core = lax.rem(t, 2)
    other = 1 - core
    chip = t // 2
    x, y = chip // 4, lax.rem(chip, 4)

    def chip_at(dx, dy):
        return lax.rem(x + dx, 4) * 4 + lax.rem(y + dy, 4)

    def plane(dx, dy):
        return (z, chip_at(dx, dy) * 2 + core)

    def depth(dz):
        return (lax.rem(z + dz, 4), t)

    sibling = (z, chip * 2 + other)
    started = []

    def send(src, dst, send_sem, recv_sem, device):
        copy = pltpu.make_async_remote_copy(
            src_ref=src, dst_ref=dst, send_sem=send_sem, recv_sem=recv_sem, device_id=device, device_id_type=MESH
        )
        copy.start()
        started.append(copy)
        return copy

    def landed(ref, sem):
        pltpu.make_async_copy(ref, ref, sem).wait()

    q_load = pltpu.make_async_copy(q_init, q_vm, q_load_sem)
    q_load.start()
    loads = []
    size = 256 // LOADS
    for m in range(2):
        for i in range(LOADS):
            rows = pl.ds(i * size, size)
            k = (m * LOADS + i) * 2
            pair = (
                pltpu.make_async_copy(grads.at[0, m, rows], merged.at[m, rows], load_sem.at[k]),
                pltpu.make_async_copy(error.at[0, m, rows], error_vm.at[m, rows], load_sem.at[k + 1]),
            )
            for copy in pair:
                copy.start()
            loads.append((m, rows, pair))

    barrier = pltpu.get_barrier_semaphore()
    peers = [plane(dx, dy) for dx, dy in FAR_FIRST] + [depth(dz) for dz in (2, 1, 3)] + [sibling]
    for peer in peers:
        pl.semaphore_signal(barrier, inc=1, device_id=peer, device_id_type=MESH)

    q_load.wait()
    half = pl.ds(pl.multiple_of(core * 256, 256), 256)
    right_in[0, core, chip, :, half] = q_vm[core].astype(BF)
    q_stage[...] = q_vm[other].astype(BF)
    pl.semaphore_wait(barrier, len(peers))
    send(q_stage, right_in.at[0, other, chip, :, half], q_core_sem.at[0], q_core_sem.at[1], sibling)

    def rights(stage):
        return right_in.at[stage] if stage < 2 else right_out

    def gather(stage, use):
        right = rights(stage)
        block = right.at[core, chip]
        for k, (dx, dy) in enumerate(FAR_FIRST):
            send(block, block, ag_send.at[stage, k], ag_recv.at[stage, k], plane(dx, dy))
        send(block, block, fwd_send.at[stage, 15], fwd_recv.at[stage, 15], sibling)
        use(core, chip)
        behind = [(15, chip)]

        def take():
            k, p = behind.pop(0)
            landed(right.at[other, p], fwd_recv.at[stage, k])
            use(other, p)

        for dx, dy in NEAR_FIRST:
            k = FAR_FIRST.index((dx, dy))
            p = chip_at(4 - dx, 4 - dy)
            block = right.at[core, p]
            landed(block, ag_recv.at[stage, k])
            send(block, block, fwd_send.at[stage, k], fwd_recv.at[stage, k], sibling)
            use(core, p)
            behind.append((k, p))
            if len(behind) > 2:
                take()
        while behind:
            take()

    for m, rows, pair in loads:
        for copy in pair:
            copy.wait()
        merged[m, rows] = (merged[m, rows].astype(F32) + error_vm[m, rows].astype(F32)).astype(BF)

    got = right_in.at[0, core, chip, :, pl.ds(pl.multiple_of(other * 256, 256), 256)]
    landed(got, q_core_sem.at[1])

    for sweep in range(ITERS):
        acc = {True: jnp.zeros((32, 256), F32), False: jnp.zeros((32, 256), F32)}
        right = rights(sweep)

        def add_left(m, p):
            cols = pl.ds(pl.multiple_of(p * 512, 512), 512)
            acc[m is core] += nt(right[m, p], merged[m, :, cols])

        gather(sweep, add_left)
        left_part[sweep, z, core] = acc[True].astype(BF)
        left_part[sweep, z, other] = acc[False].astype(BF)

        own = left_part.at[sweep, z]
        for k, dz in enumerate((2, 1, 3)):
            send(own, own, left_send.at[sweep, k], left_recv.at[sweep], depth(dz))
        landed(left_part.at[sweep, pl.ds(0, 3)], left_recv.at[sweep])
        for m in range(2):
            total = left_part[sweep, 0, m].astype(F32)
            for k in range(1, 4):
                total += left_part[sweep, k, m].astype(F32)
            left_sum[m] = total
            left_bf[m] = total.astype(BF)

        for m in range(2):
            gram_own[sweep, m, :, 0:32] = nt(left_sum[m], left_sum[m], precision=HIGHEST)
            gram_own[sweep, m, :, 32:128] = jnp.zeros((32, 96), F32)
        send(gram_own.at[sweep, other], gram_core.at[sweep], gc_sem.at[sweep, 0], gc_sem.at[sweep, 1], sibling)

        for j, dx in enumerate(RING):
            first = lax.rem(x + dx, 4) * 4
            for i in range(4):
                cols = pl.ds(pl.multiple_of((first + i) * 512, 512), 512)
                part[sweep, first + i] = nn(left_bf[other], merged[other, :, cols]).astype(BF)
            blocks = pl.ds(first, 4)
            send(part.at[sweep, blocks], part_in.at[sweep, blocks], core_send.at[sweep, j], core_recv.at[sweep, j], sibling)
        for j, dx in enumerate(RING):
            first = lax.rem(x + dx, 4) * 4
            partial = []
            for i in range(4):
                cols = pl.ds(pl.multiple_of((first + i) * 512, 512), 512)
                partial.append(nn(left_bf[core], merged[core, :, cols]))
            landed(part_in.at[sweep, pl.ds(first, 4)], core_recv.at[sweep, j])
            for i in range(4):
                chip_sum[sweep, first + i] = (partial[i] + part_in[sweep, first + i].astype(F32)).astype(BF)
            for dy in RING:
                if (dx, dy) != (0, 0):
                    k = FAR_FIRST.index((dx, dy))
                    send(
                        chip_sum.at[sweep, chip_at(dx, dy)], plane_in.at[sweep, chip],
                        rs_send.at[sweep, k], rs_recv.at[sweep], plane(dx, dy),
                    )
            if j == 0:
                landed(gram_core.at[sweep], gc_sem.at[sweep, 1])
                gram = gram_own[sweep, core] + gram_core[sweep]
                packed = gram[0:8]
                for i in range(1, 4):
                    packed += pltpu.roll(gram[i * 8 : i * 8 + 8], 32 * i, 1)
                gram_in[sweep, chip] = packed
                for k, (ex, ey) in enumerate(FAR_FIRST):
                    send(gram_in.at[sweep, chip], gram_in.at[sweep, chip], g_send.at[sweep, k], g_recv.at[sweep], plane(ex, ey))
        plane_in[sweep, chip] = chip_sum[sweep, chip]

        landed(plane_in.at[sweep, pl.ds(0, 15)], rs_recv.at[sweep])
        total = plane_in[sweep, 0].astype(F32)
        for p in range(1, 16):
            total += plane_in[sweep, p].astype(F32)
        z_in[sweep, z] = total.astype(BF)
        own = z_in.at[sweep, z]
        for k, dz in enumerate((2, 1, 3)):
            send(own, own, z_send.at[sweep, k], z_recv.at[sweep], depth(dz))

        landed(gram_in.at[sweep, pl.ds(0, 15)], g_recv.at[sweep])
        packed = gram_in[sweep, 0]
        for p in range(1, 16):
            packed += gram_in[sweep, p]
        lane = lax.broadcasted_iota(jnp.int32, (8, 128), 1)
        lines = [packed] + [pltpu.roll(packed, 128 - 32 * i, 1) for i in range(1, 4)]
        gram = jnp.concatenate([jnp.where(lane < 32, line, 0.0) for line in lines], axis=0)
        inverse = inverse_factor(gram)

        landed(z_in.at[sweep, pl.ds(0, 3)], z_recv.at[sweep])
        total = z_in[sweep, 0].astype(F32)
        for k in range(1, 4):
            total += z_in[sweep, k].astype(F32)
        rights(sweep + 1)[core, chip] = (nn(inverse, total, precision=HIGHEST) * 0.25).astype(BF)

        if sweep == ITERS - 1:
            inv_own[core, :, 0:32] = inverse
            inv_own[core, :, 32:128] = jnp.zeros((32, 96), F32)
            mine = inv_own.at[core]
            send(mine, mine, inv_sem.at[0], inv_sem.at[1], sibling)

    gather(ITERS, lambda m, p: None)
    landed(inv_own.at[other], inv_sem.at[1])
    for m in range(2):
        basis_out[m] = nn(inv_own[m, :, 0:32], left_sum[m], precision=HIGHEST)
    for copy in started:
        copy.wait_send()


def apply_kernel(merged, right, basis, new_error, p_factor, q_factor, out_vm, sem):
    chip = lax.axis_index("tensor") // 2
    core = lax.rem(lax.axis_index("tensor"), 2)
    copies = []
    for m in range(2):
        high = basis[m].astype(BF)
        low = (basis[m] - high.astype(F32)).astype(BF)
        both = jnp.concatenate([high, low], axis=0)
        for p in range(16):
            block = jnp.concatenate([right[m, p], right[m, p]], axis=0)
            cols = pl.ds(p * 512, 512)
            low_rank = lax.dot_general(both, block, (((0,), (0,)), ((), ())), preferred_element_type=F32)
            out_vm[m, :, cols] = (merged[m, :, cols].astype(F32) - low_rank).astype(BF)
            if p % 4 == 3:
                cols = pl.ds((p - 3) * 512, 2048)
                copy = pltpu.make_async_copy(out_vm.at[m, :, cols], new_error.at[0, m, :, cols], sem.at[m * 4 + p // 4])
                copy.start()
                copies.append(copy)
        p_factor[m] = basis[m] * math.sqrt(8192)
        q_factor[m] = right[m, chip, :, pl.ds(pl.multiple_of(core * 256, 256), 256)].astype(F32)
    for copy in copies:
        copy.wait()


def local(grads, error, q_init):
    hbm = pl.BlockSpec(memory_space=pltpu.HBM)
    vmem = pl.BlockSpec(memory_space=pltpu.VMEM)
    dma = pltpu.SemaphoreType.DMA
    merged, right, basis = pl.pallas_call(
        factors_kernel,
        name="factors",
        out_shape=(
            pltpu.VMEM((2, 256, 8192), BF),
            pltpu.VMEM((2, 16, 32, 512), BF),
            pltpu.VMEM((2, 32, 256), F32),
        ),
        in_specs=[hbm] * 3,
        out_specs=(vmem,) * 3,
        scratch_shapes=[
            pltpu.VMEM((2, 256, 8192), BF),
            pltpu.VMEM((2, 32, 256), F32),
            pltpu.VMEM((2, 2, 16, 32, 512), BF),
            pltpu.VMEM((2, 4, 2, 32, 256), BF),
            pltpu.VMEM((2, 32, 256), F32),
            pltpu.VMEM((2, 32, 256), BF),
            pltpu.VMEM((2, 16, 32, 512), BF),
            pltpu.VMEM((2, 16, 32, 512), BF),
            pltpu.VMEM((2, 16, 32, 512), BF),
            pltpu.VMEM((2, 16, 32, 512), BF),
            pltpu.VMEM((2, 4, 32, 512), BF),
            pltpu.VMEM((2, 2, 32, 128), F32),
            pltpu.VMEM((2, 32, 128), F32),
            pltpu.VMEM((2, 16, 8, 128), F32),
            pltpu.VMEM((2, 32, 128), F32),
            pltpu.VMEM((32, 256), BF),
            dma((4 * LOADS,)), dma, dma((2,)),
            dma((3, 15)), dma((3, 15)), dma((3, 16)), dma((3, 16)),
            dma((2, 3)), dma((2,)), dma((2, 4)), dma((2, 4)), dma((2, 15)), dma((2,)), dma((2, 3)), dma((2,)),
            dma((2, 2)), dma((2, 15)), dma((2,)), dma((2,)),
        ],
        compiler_params=pltpu.CompilerParams(
            collective_id=0, has_side_effects=True, vmem_limit_bytes=32 << 20
        ),
    )(
        pltpu.with_memory_space_constraint(grads, pltpu.HBM),
        pltpu.with_memory_space_constraint(error, pltpu.HBM),
        q_init.transpose(0, 2, 1),
    )
    new_error, p_factor, q_factor = pl.pallas_call(
        apply_kernel,
        name="apply",
        out_shape=(
            jax.ShapeDtypeStruct((1, 2, 256, 8192), BF),
            jax.ShapeDtypeStruct((2, 32, 256), F32),
            jax.ShapeDtypeStruct((2, 32, 256), F32),
        ),
        in_specs=[vmem] * 3,
        out_specs=(hbm, vmem, vmem),
        scratch_shapes=[pltpu.VMEM((2, 256, 8192), BF), dma((8,))],
        compiler_params=pltpu.CompilerParams(vmem_limit_bytes=24 << 20),
    )(merged, right, basis)
    return new_error, p_factor.transpose(0, 2, 1), q_factor.transpose(0, 2, 1)


def solution(mesh):
    in_specs = (
        P("dp", None, "tensor", None),
        P("dp", None, "tensor", None),
        P(None, "tensor", None),
    )
    out_specs = (P("dp", None, "tensor", None), P(None, "tensor", None), P(None, "tensor", None))
    return jax.shard_map(local, mesh=mesh, in_specs=in_specs, out_specs=out_specs, check_vma=False)
```

```python
import math

import jax
import jax.numpy as jnp
from jax import lax
from jax.experimental import pallas as pl
from jax.experimental.pallas import tpu as pltpu
from jax.sharding import PartitionSpec as P

ITERS = 2
BF = jnp.bfloat16
F32 = jnp.float32
MESH = pl.DeviceIdType.MESH
HIGHEST = lax.Precision.HIGHEST
FAR_FIRST = tuple(
    sorted(
        ((dx, dy) for dx in range(4) for dy in range(4) if dx or dy),
        key=lambda s: -(min(s[0], 4 - s[0]) + min(s[1], 4 - s[1])),
    )
)
NEAR_FIRST = FAR_FIRST[::-1]
LOADS = 4
PANEL = 16


def nt(a, b, **kw):
    return lax.dot_general(a, b, (((1,), (1,)), ((), ())), preferred_element_type=F32, **kw)


def nn(a, b, **kw):
    return lax.dot_general(a, b, (((1,), (0,)), ((), ())), preferred_element_type=F32, **kw)


def inverse_factor(gram):
    n = gram.shape[0]
    row = lax.broadcasted_iota(jnp.int32, (n, 4 * n), 0)
    lane = lax.broadcasted_iota(jnp.int32, (n, 4 * n), 1)
    work = jnp.where(lane == row + n, 1.0, gram)
    for first in range(0, n, PANEL):
        spread = [jnp.broadcast_to(work[:, first + i : first + i + 1], work.shape) for i in range(PANEL)]
        for i in range(PANEL):
            j = first + i
            share = jnp.where(row > j, spread[i] * (1.0 / spread[i][j : j + 1, :]), 0.0)
            for k in range(i + 1, PANEL):
                spread[k] = spread[k] - share * spread[k][j : j + 1, :]
            work = work - share * work[j : j + 1, :]
    diagonal = jnp.sum(jnp.where(lane == row, work, 0.0), axis=1, keepdims=True)
    work = work * lax.rsqrt(diagonal)
    return work[:, n : 2 * n]


def factors_kernel(
    grads, error, q_init, rest, p_out, q_out,
    merged, sibling_rows, q_vm, q_stage, right_in, right_last, left_part, left_sum, left_bf,
    chip_sum, plane_in, z_in, gram_pad, gram_in, basis, basis_stage, basis_t,
    load_sem, q_load_sem, q_core_sem, swap_send, swap_recv, ag_send, ag_recv, fwd_send, fwd_recv,
    left_send, left_recv, rs_send, rs_recv, z_send, z_recv, g_send, g_recv, basis_sem,
):
    z = lax.axis_index("dp")
    t = lax.axis_index("tensor")
    core = lax.rem(t, 2)
    other = 1 - core
    chip = t // 2
    x, y = chip // 4, lax.rem(chip, 4)

    def chip_at(dx, dy):
        return lax.rem(x + dx, 4) * 4 + lax.rem(y + dy, 4)

    def plane(dx, dy):
        return (z, chip_at(dx, dy) * 2 + core)

    def depth(dz):
        return (lax.rem(z + dz, 4), t)

    sibling = (z, chip * 2 + other)
    started = []

    def send(src, dst, send_sem, recv_sem, device):
        copy = pltpu.make_async_remote_copy(
            src_ref=src, dst_ref=dst, send_sem=send_sem, recv_sem=recv_sem, device_id=device, device_id_type=MESH
        )
        copy.start()
        started.append(copy)

    def landed(ref, sem):
        pltpu.make_async_copy(ref, ref, sem).wait()

    def columns(p, h):
        return pl.ds(pl.multiple_of(p * 512 + h * 256, 256), 256)

    q_load = pltpu.make_async_copy(q_init, q_vm, q_load_sem)
    q_load.start()
    loads = []
    size = 256 // LOADS
    for m in range(2):
        for i in range(LOADS):
            which = (other, core)[m]
            rows = pl.ds(i * size, size)
            k = (m * LOADS + i) * 2
            pair = (
                pltpu.make_async_copy(grads.at[0, which, rows], merged.at[which, rows], load_sem.at[k]),
                pltpu.make_async_copy(error.at[0, which, rows], rest.at[which, rows], load_sem.at[k + 1]),
            )
            for copy in pair:
                copy.start()
            loads.append((which, rows, pair))

    barrier = pltpu.get_barrier_semaphore()
    peers = [plane(dx, dy) for dx, dy in FAR_FIRST] + [depth(dz) for dz in (2, 1, 3)] + [sibling]
    for peer in peers:
        pl.semaphore_signal(barrier, inc=1, device_id=peer, device_id_type=MESH)

    def merge(which, rows, pair):
        for copy in pair:
            copy.wait()
        merged[which, rows] = (merged[which, rows].astype(F32) + rest[which, rows].astype(F32)).astype(BF)

    def gather(stage, h, right):
        for k, (dx, dy) in enumerate(FAR_FIRST):
            send(right.at[h, chip], right.at[h, chip], ag_send.at[stage, h, k], ag_recv.at[stage, h, k], plane(dx, dy))

    def arrivals(stage, h, right):
        yield 15, chip
        for dx, dy in NEAR_FIRST:
            k = FAR_FIRST.index((dx, dy))
            p = chip_at(4 - dx, 4 - dy)
            landed(right.at[h, p], ag_recv.at[stage, h, k])
            yield k, p

    q_load.wait()
    right_in[0, core, chip] = q_vm[core].astype(BF)
    q_stage[...] = q_vm[other].astype(BF)
    for load in loads[:LOADS]:
        merge(*load)
    pl.semaphore_wait(barrier, len(peers))
    send(q_stage, right_in.at[0, core, chip], q_core_sem.at[0], q_core_sem.at[1], sibling)
    gather(0, core, right_in.at[0])
    swaps = []
    for i, (_, rows, _) in enumerate(loads[:LOADS]):
        copy = pltpu.make_async_remote_copy(
            src_ref=merged.at[other, rows], dst_ref=sibling_rows.at[rows], send_sem=swap_send.at[i],
            recv_sem=swap_recv.at[i], device_id=sibling, device_id_type=MESH,
        )
        copy.start()
        swaps.append(copy)
    landed(right_in.at[0, other, chip], q_core_sem.at[1])
    gather(0, other, right_in.at[0])
    for load in loads[LOADS:]:
        merge(*load)

    inverse = None
    for sweep in range(ITERS):
        right = right_in.at[sweep]
        own_rows = jnp.zeros((32, 256), F32)
        its_rows = jnp.zeros((32, 256), F32)
        here = []
        for i, h in enumerate((core, other) if sweep == 0 else (0, 1)):
            if sweep == 0 and i == 1:
                for copy in swaps:
                    copy.wait()
                for early, p in here:
                    its_rows += nt(right[early, p], sibling_rows[:, columns(p, early)])
            for _, p in arrivals(sweep, h, right):
                own_rows += nt(right[h, p], merged[core, :, columns(p, h)])
                if sweep == 0 and i == 0:
                    here.append((h, p))
                else:
                    its_rows += nt(right[h, p], sibling_rows[:, columns(p, h)])
        left_part[sweep, z, core] = own_rows.astype(BF)
        left_part[sweep, z, other] = its_rows.astype(BF)

        own = left_part.at[sweep, z]
        for k, dz in enumerate((2, 1, 3)):
            send(own, own, left_send.at[sweep, k], left_recv.at[sweep], depth(dz))
        landed(left_part.at[sweep, pl.ds(0, 3)], left_recv.at[sweep])
        for i in range(2):
            total = left_part[sweep, 0, i].astype(F32)
            for k in range(1, 4):
                total += left_part[sweep, k, i].astype(F32)
            left_sum[i] = total
            left_bf[i] = total.astype(BF)

        for h in range(2):
            for k, (dx, dy) in enumerate(FAR_FIRST + ((0, 0),)):
                p = chip_at(dx, dy)
                block = nn(left_bf[core], merged[core, :, columns(p, h)])
                block = (block + nn(left_bf[other], sibling_rows[:, columns(p, h)])).astype(BF)
                if k == 15:
                    plane_in[sweep, h, chip] = block
                else:
                    chip_sum[sweep, h, p] = block
                    send(
                        chip_sum.at[sweep, h, p], plane_in.at[sweep, h, chip],
                        rs_send.at[sweep, h, k], rs_recv.at[sweep, h], plane(dx, dy),
                    )
            if h == 0:
                gram_pad[:, 0:32] = nt(left_sum[0], left_sum[0], precision=HIGHEST) + nt(
                    left_sum[1], left_sum[1], precision=HIGHEST
                )
                gram_pad[:, 32:128] = jnp.zeros((32, 96), F32)
                packed = gram_pad[0:8]
                for i in range(1, 4):
                    packed += pltpu.roll(gram_pad[i * 8 : i * 8 + 8], 32 * i, 1)
                gram_in[sweep, chip] = packed
                for k, (dx, dy) in enumerate(FAR_FIRST):
                    send(gram_in.at[sweep, chip], gram_in.at[sweep, chip], g_send.at[sweep, k], g_recv.at[sweep], plane(dx, dy))

        for h in range(2):
            landed(plane_in.at[sweep, h, pl.ds(0, 15)], rs_recv.at[sweep, h])
            total = plane_in[sweep, h, 0].astype(F32)
            for p in range(1, 16):
                total += plane_in[sweep, h, p].astype(F32)
            z_in[sweep, h, z] = total.astype(BF)
            own = z_in.at[sweep, h, z]
            for k, dz in enumerate((2, 1, 3)):
                send(own, own, z_send.at[sweep, h, k], z_recv.at[sweep, h], depth(dz))
            if h == 0:
                landed(gram_in.at[sweep, pl.ds(0, 15)], g_recv.at[sweep])
                packed = gram_in[sweep, 0]
                for p in range(1, 16):
                    packed += gram_in[sweep, p]
                lane = lax.broadcasted_iota(jnp.int32, (8, 128), 1)
                lines = [packed] + [pltpu.roll(packed, 128 - 32 * i, 1) for i in range(1, 4)]
                gram = jnp.concatenate([jnp.where(lane < 32, line, 0.0) for line in lines], axis=0)
                inverse = inverse_factor(gram)
        if sweep == ITERS - 1:
            basis_stage[...] = nn(inverse, left_sum[other], precision=HIGHEST)
            send(basis_stage, basis.at[core], basis_sem.at[0], basis_sem.at[1], sibling)
            basis[core] = nn(inverse, left_sum[core], precision=HIGHEST)
        sent = started[:]
        started.clear()
        after = right_in.at[sweep + 1] if sweep < ITERS - 1 else right_last.at[core]
        for h in range(2):
            landed(z_in.at[sweep, h, pl.ds(0, 3)], z_recv.at[sweep, h])
            total = z_in[sweep, h, 0].astype(F32)
            for k in range(1, 4):
                total += z_in[sweep, h, k].astype(F32)
            after[h, chip] = (nn(inverse, total, precision=HIGHEST) * 0.25).astype(BF)
            gather(sweep + 1, h, after)
        for copy in sent:
            copy.wait_send()

    landed(basis.at[other], basis_sem.at[1])
    factor = []
    for m in range(2):
        p_out[m] = basis[m] * math.sqrt(8192)
        tall = basis[m].T
        high = tall.astype(BF)
        low = (tall - high.astype(F32)).astype(BF)
        factor.append(jnp.concatenate([high, low], axis=1))
    basis_t[0], basis_t[1] = factor

    def subtract(m, h, p):
        block = right_last[m, h, p]
        low_rank = nn(basis_t[m], jnp.concatenate([block, block], axis=0))
        cols = columns(p, h)
        rest[m, :, cols] = (merged[m, :, cols].astype(F32) - low_rank).astype(BF)

    behind = []

    def take():
        group = behind.pop(0)
        for h, k, p in group:
            landed(right_last.at[other, h, p], fwd_recv.at[h, k])
        for h, _, p in group:
            subtract(other, h, p)

    for h in range(2):
        coming = arrivals(ITERS, h, right_last.at[core])
        for _ in range(4):
            group = []
            for _ in range(4):
                k, p = next(coming)
                block = right_last.at[core, h, p]
                send(block, block, fwd_send.at[h, k], fwd_recv.at[h, k], sibling)
                group.append((h, k, p))
            for _, _, p in group:
                subtract(core, h, p)
            behind.append(group)
            if len(behind) > 4:
                take()
    while behind:
        take()
    for m in range(2):
        q_out[m] = right_last[m, core, chip].astype(F32)
    for copy in started:
        copy.wait_send()


def store_kernel(rest, p_in, q_in, new_error, p_factor, q_factor, sem):
    copies = [
        pltpu.make_async_copy(p_in, p_factor, sem.at[16]),
        pltpu.make_async_copy(q_in, q_factor, sem.at[17]),
    ]
    for m in range(2):
        for i in range(8):
            rows = pl.ds(i * 32, 32)
            copies.append(pltpu.make_async_copy(rest.at[m, rows], new_error.at[0, m, rows], sem.at[m * 8 + i]))
    for copy in copies:
        copy.start()
    for copy in copies:
        copy.wait()


def local(grads, error, q_init):
    hbm = pl.BlockSpec(memory_space=pltpu.HBM)
    vmem = pl.BlockSpec(memory_space=pltpu.VMEM)
    dma = pltpu.SemaphoreType.DMA
    rest, p_factor, q_factor = pl.pallas_call(
        factors_kernel,
        name="factors",
        out_shape=(
            pltpu.VMEM((2, 256, 8192), BF),
            pltpu.VMEM((2, 32, 256), F32),
            pltpu.VMEM((2, 32, 256), F32),
        ),
        in_specs=[hbm] * 3,
        out_specs=(vmem,) * 3,
        scratch_shapes=[
            pltpu.VMEM((2, 256, 8192), BF),
            pltpu.VMEM((256, 8192), BF),
            pltpu.VMEM((2, 32, 256), F32),
            pltpu.VMEM((32, 256), BF),
            pltpu.VMEM((2, 2, 16, 32, 256), BF),
            pltpu.VMEM((2, 2, 16, 32, 256), BF),
            pltpu.VMEM((2, 4, 2, 32, 256), BF),
            pltpu.VMEM((2, 32, 256), F32),
            pltpu.VMEM((2, 32, 256), BF),
            pltpu.VMEM((2, 2, 16, 32, 256), BF),
            pltpu.VMEM((2, 2, 16, 32, 256), BF),
            pltpu.VMEM((2, 2, 4, 32, 256), BF),
            pltpu.VMEM((32, 128), F32),
            pltpu.VMEM((2, 16, 8, 128), F32),
            pltpu.VMEM((2, 32, 256), F32),
            pltpu.VMEM((32, 256), F32),
            pltpu.VMEM((2, 256, 64), BF),
            dma((4 * LOADS,)), dma, dma((2,)), dma((LOADS,)), dma((LOADS,)),
            dma((3, 2, 15)), dma((3, 2, 15)), dma((2, 16)), dma((2, 16)),
            dma((2, 3)), dma((2,)), dma((2, 2, 15)), dma((2, 2)), dma((2, 2, 3)), dma((2, 2)),
            dma((2, 15)), dma((2,)), dma((2,)),
        ],
        compiler_params=pltpu.CompilerParams(
            collective_id=0, has_side_effects=True, vmem_limit_bytes=32 << 20
        ),
    )(
        pltpu.with_memory_space_constraint(grads, pltpu.HBM),
        pltpu.with_memory_space_constraint(error, pltpu.HBM),
        pltpu.with_memory_space_constraint(q_init.transpose(0, 2, 1), pltpu.HBM),
    )
    new_error, p_factor, q_factor = pl.pallas_call(
        store_kernel,
        name="store",
        out_shape=(
            pltpu.HBM((1, 2, 256, 8192), BF),
            pltpu.HBM((2, 32, 256), F32),
            pltpu.HBM((2, 32, 256), F32),
        ),
        in_specs=[vmem] * 3,
        out_specs=(hbm,) * 3,
        scratch_shapes=[dma((18,))],
        compiler_params=pltpu.CompilerParams(vmem_limit_bytes=24 << 20),
    )(rest, p_factor, q_factor)
    return new_error, p_factor.transpose(0, 2, 1), q_factor.transpose(0, 2, 1)


def solution(mesh):
    in_specs = (
        P("dp", None, "tensor", None),
        P("dp", None, "tensor", None),
        P(None, "tensor", None),
    )
    out_specs = (P("dp", None, "tensor", None), P(None, "tensor", None), P(None, "tensor", None))
    return jax.shard_map(local, mesh=mesh, in_specs=in_specs, out_specs=out_specs, check_vma=False)
```

```python
import math

import jax
import jax.numpy as jnp
from jax import lax
from jax.experimental import pallas as pl
from jax.experimental.pallas import tpu as pltpu
from jax.sharding import PartitionSpec as P

ITERS = 2
BF = jnp.bfloat16
F32 = jnp.float32
MESH = pl.DeviceIdType.MESH
HIGHEST = lax.Precision.HIGHEST
FAR_FIRST = tuple(
    sorted(
        ((dx, dy) for dx in range(4) for dy in range(4) if dx or dy),
        key=lambda s: -(min(s[0], 4 - s[0]) + min(s[1], 4 - s[1])),
    )
)
NEAR_FIRST = FAR_FIRST[::-1]
LOADS = 4
PANEL = 16


def nt(a, b, **kw):
    return lax.dot_general(a, b, (((1,), (1,)), ((), ())), preferred_element_type=F32, **kw)


def nn(a, b, **kw):
    return lax.dot_general(a, b, (((1,), (0,)), ((), ())), preferred_element_type=F32, **kw)


def inverse_factor(gram):
    n = gram.shape[0]
    row = lax.broadcasted_iota(jnp.int32, (n, 4 * n), 0)
    lane = lax.broadcasted_iota(jnp.int32, (n, 4 * n), 1)
    work = jnp.where(lane == row + n, 1.0, gram)
    for first in range(0, n, PANEL):
        spread = [jnp.broadcast_to(work[:, first + i : first + i + 1], work.shape) for i in range(PANEL)]
        for i in range(PANEL):
            j = first + i
            share = jnp.where(row > j, spread[i] * (1.0 / spread[i][j : j + 1, :]), 0.0)
            for k in range(i + 1, PANEL):
                spread[k] = spread[k] - share * spread[k][j : j + 1, :]
            work = work - share * work[j : j + 1, :]
    diagonal = jnp.sum(jnp.where(lane == row, work, 0.0), axis=1, keepdims=True)
    work = work * lax.rsqrt(diagonal)
    return work[:, n : 2 * n]


def factors_kernel(
    grads, error, q_init, rest, p_out, q_out,
    merged, sibling_rows, q_vm, q_stage, right_in, right_last, left_part, left_sum, left_bf,
    chip_sum, plane_in, z_in, gram_pad, gram_in, basis, basis_stage, basis_t,
    load_sem, q_load_sem, q_core_sem, swap_send, swap_recv, ag_send, ag_recv, fwd_send, fwd_recv,
    left_send, left_recv, rs_send, rs_recv, z_send, z_recv, g_send, g_recv, basis_sem,
):
    z = lax.axis_index("dp")
    t = lax.axis_index("tensor")
    core = lax.rem(t, 2)
    other = 1 - core
    chip = t // 2
    x, y = chip // 4, lax.rem(chip, 4)

    def chip_at(dx, dy):
        return lax.rem(x + dx, 4) * 4 + lax.rem(y + dy, 4)

    def plane(dx, dy):
        return (z, chip_at(dx, dy) * 2 + core)

    def depth(dz):
        return (lax.rem(z + dz, 4), t)

    sibling = (z, chip * 2 + other)
    started = []

    def send(src, dst, send_sem, recv_sem, device):
        copy = pltpu.make_async_remote_copy(
            src_ref=src, dst_ref=dst, send_sem=send_sem, recv_sem=recv_sem, device_id=device, device_id_type=MESH
        )
        copy.start()
        started.append(copy)

    def landed(ref, sem):
        pltpu.make_async_copy(ref, ref, sem).wait()

    def columns(p, h):
        return pl.ds(pl.multiple_of(p * 512 + h * 256, 256), 256)

    q_load = pltpu.make_async_copy(q_init, q_vm, q_load_sem)
    q_load.start()
    loads = []
    size = 256 // LOADS
    for m in range(2):
        for i in range(LOADS):
            which = (other, core)[m]
            rows = pl.ds(i * size, size)
            k = (m * LOADS + i) * 2
            pair = (
                pltpu.make_async_copy(grads.at[0, which, rows], merged.at[which, rows], load_sem.at[k]),
                pltpu.make_async_copy(error.at[0, which, rows], rest.at[which, rows], load_sem.at[k + 1]),
            )
            for copy in pair:
                copy.start()
            loads.append((which, rows, pair))

    barrier = pltpu.get_barrier_semaphore()
    peers = [plane(dx, dy) for dx, dy in FAR_FIRST] + [depth(dz) for dz in (2, 1, 3)] + [sibling]
    for peer in peers:
        pl.semaphore_signal(barrier, inc=1, device_id=peer, device_id_type=MESH)

    def merge(which, rows, pair):
        for copy in pair:
            copy.wait()
        merged[which, rows] = (merged[which, rows].astype(F32) + rest[which, rows].astype(F32)).astype(BF)

    def gather(stage, h, right):
        for k, (dx, dy) in enumerate(FAR_FIRST):
            send(right.at[h, chip], right.at[h, chip], ag_send.at[stage, h, k], ag_recv.at[stage, h, k], plane(dx, dy))

    def arrivals(stage, h, right):
        yield 15, chip
        for dx, dy in NEAR_FIRST:
            k = FAR_FIRST.index((dx, dy))
            p = chip_at(4 - dx, 4 - dy)
            landed(right.at[h, p], ag_recv.at[stage, h, k])
            yield k, p

    q_load.wait()
    right_in[0, core, chip] = q_vm[core].astype(BF)
    q_stage[...] = q_vm[other].astype(BF)
    for load in loads[:LOADS]:
        merge(*load)
    pl.semaphore_wait(barrier, len(peers))
    send(q_stage, right_in.at[0, core, chip], q_core_sem.at[0], q_core_sem.at[1], sibling)
    gather(0, core, right_in.at[0])
    swaps = []
    for i, (_, rows, _) in enumerate(loads[:LOADS]):
        copy = pltpu.make_async_remote_copy(
            src_ref=merged.at[other, rows], dst_ref=sibling_rows.at[rows], send_sem=swap_send.at[i],
            recv_sem=swap_recv.at[i], device_id=sibling, device_id_type=MESH,
        )
        copy.start()
        swaps.append(copy)
    landed(right_in.at[0, other, chip], q_core_sem.at[1])
    gather(0, other, right_in.at[0])
    for load in loads[LOADS:]:
        merge(*load)

    inverse = None
    for sweep in range(ITERS):
        right = right_in.at[sweep]
        own_rows = jnp.zeros((32, 256), F32)
        its_rows = jnp.zeros((32, 256), F32)
        here = []
        for i, h in enumerate((core, other) if sweep == 0 else (0, 1)):
            if sweep == 0 and i == 1:
                for copy in swaps:
                    copy.wait()
                for early, p in here:
                    its_rows += nt(right[early, p], sibling_rows[:, columns(p, early)])
            for _, p in arrivals(sweep, h, right):
                own_rows += nt(right[h, p], merged[core, :, columns(p, h)])
                if sweep == 0 and i == 0:
                    here.append((h, p))
                else:
                    its_rows += nt(right[h, p], sibling_rows[:, columns(p, h)])
        left_part[sweep, z, core] = own_rows.astype(BF)
        left_part[sweep, z, other] = its_rows.astype(BF)

        own = left_part.at[sweep, z]
        for k, dz in enumerate((2, 1, 3)):
            send(own, own, left_send.at[sweep, k], left_recv.at[sweep], depth(dz))
        landed(left_part.at[sweep, pl.ds(0, 3)], left_recv.at[sweep])
        for i in range(2):
            total = left_part[sweep, 0, i].astype(F32)
            for k in range(1, 4):
                total += left_part[sweep, k, i].astype(F32)
            left_sum[i] = total
            left_bf[i] = total.astype(BF)

        for h in range(2):
            for k, (dx, dy) in enumerate(FAR_FIRST + ((0, 0),)):
                p = chip_at(dx, dy)
                block = nn(left_bf[core], merged[core, :, columns(p, h)])
                block = (block + nn(left_bf[other], sibling_rows[:, columns(p, h)])).astype(BF)
                if k == 15:
                    plane_in[sweep, h, chip] = block
                else:
                    chip_sum[sweep, h, p] = block
                    send(
                        chip_sum.at[sweep, h, p], plane_in.at[sweep, h, chip],
                        rs_send.at[sweep, h, k], rs_recv.at[sweep, h], plane(dx, dy),
                    )
            if h == 0:
                gram_pad[:, 0:32] = nt(left_sum[0], left_sum[0], precision=HIGHEST) + nt(
                    left_sum[1], left_sum[1], precision=HIGHEST
                )
                gram_pad[:, 32:128] = jnp.zeros((32, 96), F32)
                packed = gram_pad[0:8]
                for i in range(1, 4):
                    packed += pltpu.roll(gram_pad[i * 8 : i * 8 + 8], 32 * i, 1)
                gram_in[sweep, chip] = packed
                for k, (dx, dy) in enumerate(FAR_FIRST):
                    send(gram_in.at[sweep, chip], gram_in.at[sweep, chip], g_send.at[sweep, k], g_recv.at[sweep], plane(dx, dy))

        sent = started[:]
        started.clear()
        for h in range(2):
            landed(plane_in.at[sweep, h, pl.ds(0, 15)], rs_recv.at[sweep, h])
            total = plane_in[sweep, h, 0].astype(F32)
            for p in range(1, 16):
                total += plane_in[sweep, h, p].astype(F32)
            z_in[sweep, h, z] = total.astype(BF)
            own = z_in.at[sweep, h, z]
            for k, dz in enumerate((2, 1, 3)):
                send(own, own, z_send.at[sweep, h, k], z_recv.at[sweep, h], depth(dz))
            if h == 0:
                landed(gram_in.at[sweep, pl.ds(0, 15)], g_recv.at[sweep])
                packed = gram_in[sweep, 0]
                for p in range(1, 16):
                    packed += gram_in[sweep, p]
                lane = lax.broadcasted_iota(jnp.int32, (8, 128), 1)
                lines = [packed] + [pltpu.roll(packed, 128 - 32 * i, 1) for i in range(1, 4)]
                gram = jnp.concatenate([jnp.where(lane < 32, line, 0.0) for line in lines], axis=0)
                inverse = inverse_factor(gram)
        if sweep == ITERS - 1:
            basis_stage[...] = nn(inverse, left_sum[other], precision=HIGHEST)
            send(basis_stage, basis.at[core], basis_sem.at[0], basis_sem.at[1], sibling)
            basis[core] = nn(inverse, left_sum[core], precision=HIGHEST)
        for copy in sent:
            copy.wait_send()
        after = right_in.at[sweep + 1] if sweep < ITERS - 1 else right_last.at[core]
        for h in range(2):
            landed(z_in.at[sweep, h, pl.ds(0, 3)], z_recv.at[sweep, h])
            total = z_in[sweep, h, 0].astype(F32)
            for k in range(1, 4):
                total += z_in[sweep, h, k].astype(F32)
            after[h, chip] = (nn(inverse, total, precision=HIGHEST) * 0.25).astype(BF)
            gather(sweep + 1, h, after)

    landed(basis.at[other], basis_sem.at[1])
    factor = []
    for m in range(2):
        p_out[m] = basis[m] * math.sqrt(8192)
        tall = basis[m].T
        high = tall.astype(BF)
        low = (tall - high.astype(F32)).astype(BF)
        factor.append(jnp.concatenate([high, low], axis=1))
    basis_t[0], basis_t[1] = factor

    def subtract(m, h, p):
        block = right_last[m, h, p]
        low_rank = nn(basis_t[m], jnp.concatenate([block, block], axis=0))
        cols = columns(p, h)
        rest[m, :, cols] = (merged[m, :, cols].astype(F32) - low_rank).astype(BF)

    behind = []

    def take():
        group = behind.pop(0)
        for h, k, p in group:
            landed(right_last.at[other, h, p], fwd_recv.at[h, k])
        for h, _, p in group:
            subtract(other, h, p)

    for h in range(2):
        coming = arrivals(ITERS, h, right_last.at[core])
        for _ in range(4):
            group = []
            for _ in range(4):
                k, p = next(coming)
                block = right_last.at[core, h, p]
                send(block, block, fwd_send.at[h, k], fwd_recv.at[h, k], sibling)
                group.append((h, k, p))
            for _, _, p in group:
                subtract(core, h, p)
            behind.append(group)
            if len(behind) > 4:
                take()
    while behind:
        take()
    for m in range(2):
        q_out[m] = right_last[m, core, chip].astype(F32)
    for copy in started:
        copy.wait_send()


def store_kernel(rest, p_in, q_in, new_error, p_factor, q_factor, sem):
    copies = [
        pltpu.make_async_copy(p_in, p_factor, sem.at[16]),
        pltpu.make_async_copy(q_in, q_factor, sem.at[17]),
    ]
    for m in range(2):
        for i in range(8):
            rows = pl.ds(i * 32, 32)
            copies.append(pltpu.make_async_copy(rest.at[m, rows], new_error.at[0, m, rows], sem.at[m * 8 + i]))
    for copy in copies:
        copy.start()
    for copy in copies:
        copy.wait()


def local(grads, error, q_init):
    hbm = pl.BlockSpec(memory_space=pltpu.HBM)
    vmem = pl.BlockSpec(memory_space=pltpu.VMEM)
    dma = pltpu.SemaphoreType.DMA
    rest, p_factor, q_factor = pl.pallas_call(
        factors_kernel,
        name="factors",
        out_shape=(
            pltpu.VMEM((2, 256, 8192), BF),
            pltpu.VMEM((2, 32, 256), F32),
            pltpu.VMEM((2, 32, 256), F32),
        ),
        in_specs=[hbm] * 3,
        out_specs=(vmem,) * 3,
        scratch_shapes=[
            pltpu.VMEM((2, 256, 8192), BF),
            pltpu.VMEM((256, 8192), BF),
            pltpu.VMEM((2, 32, 256), F32),
            pltpu.VMEM((32, 256), BF),
            pltpu.VMEM((2, 2, 16, 32, 256), BF),
            pltpu.VMEM((2, 2, 16, 32, 256), BF),
            pltpu.VMEM((2, 4, 2, 32, 256), BF),
            pltpu.VMEM((2, 32, 256), F32),
            pltpu.VMEM((2, 32, 256), BF),
            pltpu.VMEM((2, 2, 16, 32, 256), BF),
            pltpu.VMEM((2, 2, 16, 32, 256), BF),
            pltpu.VMEM((2, 2, 4, 32, 256), BF),
            pltpu.VMEM((32, 128), F32),
            pltpu.VMEM((2, 16, 8, 128), F32),
            pltpu.VMEM((2, 32, 256), F32),
            pltpu.VMEM((32, 256), F32),
            pltpu.VMEM((2, 256, 64), BF),
            dma((4 * LOADS,)), dma, dma((2,)), dma((LOADS,)), dma((LOADS,)),
            dma((3, 2, 15)), dma((3, 2, 15)), dma((2, 16)), dma((2, 16)),
            dma((2, 3)), dma((2,)), dma((2, 2, 15)), dma((2, 2)), dma((2, 2, 3)), dma((2, 2)),
            dma((2, 15)), dma((2,)), dma((2,)),
        ],
        compiler_params=pltpu.CompilerParams(
            collective_id=0, has_side_effects=True, vmem_limit_bytes=32 << 20
        ),
    )(
        pltpu.with_memory_space_constraint(grads, pltpu.HBM),
        pltpu.with_memory_space_constraint(error, pltpu.HBM),
        pltpu.with_memory_space_constraint(q_init.transpose(0, 2, 1), pltpu.HBM),
    )
    new_error, p_factor, q_factor = pl.pallas_call(
        store_kernel,
        name="store",
        out_shape=(
            pltpu.HBM((1, 2, 256, 8192), BF),
            pltpu.HBM((2, 32, 256), F32),
            pltpu.HBM((2, 32, 256), F32),
        ),
        in_specs=[vmem] * 3,
        out_specs=(hbm,) * 3,
        scratch_shapes=[dma((18,))],
        compiler_params=pltpu.CompilerParams(vmem_limit_bytes=24 << 20),
    )(rest, p_factor, q_factor)
    return new_error, p_factor.transpose(0, 2, 1), q_factor.transpose(0, 2, 1)


def solution(mesh):
    in_specs = (
        P("dp", None, "tensor", None),
        P("dp", None, "tensor", None),
        P(None, "tensor", None),
    )
    out_specs = (P("dp", None, "tensor", None), P(None, "tensor", None), P(None, "tensor", None))
    return jax.shard_map(local, mesh=mesh, in_specs=in_specs, out_specs=out_specs, check_vma=False)
```
